32 devices in a mesh: shard: 16 (over z, y, x), rep: 2 (over core).
Axes of the slice: x: 2, y: 2, z: 4, core: 2. Of those that a mesh axis runs over, the one named last changes fastest.
Arguments:
- queries_in: bfloat16 [4096, 2560], P(('shard', 'rep')), may hold values from -6 to 6
- keys_in: bfloat16 [4096, 2560], P(('shard', 'rep')), may hold values from -6 to 6
- values_in: bfloat16 [4096, 2560], P(('shard', 'rep')), may hold values from -6 to 6
- gate_z: bfloat16 [4096, 2560], P(('shard', 'rep')), may hold values from -6 to 6
- beta_logit: bfloat16 [4096, 20], P(('shard', 'rep')), may hold values from -6 to 6
- decay_in: bfloat16 [4096, 20], P(('shard', 'rep')), may hold values from -6 to 6
- a_log: float32 [20], replicated, may hold values from -4.5 to 0.5
- dt_bias: float32 [20], replicated, may hold values from -2 to 1
- conv_weight: float32 [3, 4, 2560], replicated, may hold values from -3 to 3
- norm_gain: float32 [128], replicated, may hold values from 0.1 to 1.9
- out_weight: bfloat16 [2560, 2560], P('shard'), may hold values from -0.125 to 0.125
- out_grad: bfloat16 [4096, 2560], P(('shard', 'rep')), may hold values from -6 to 6
Outputs:
- layer_out: bfloat16 [4096, 2560], P(('shard', 'rep'))
- grad_queries: bfloat16 [4096, 2560], P(('shard', 'rep'))
- grad_keys: bfloat16 [4096, 2560], P(('shard', 'rep'))
- grad_values: bfloat16 [4096, 2560], P(('shard', 'rep'))
- grad_gate: bfloat16 [4096, 2560], P(('shard', 'rep'))
- grad_beta: bfloat16 [4096, 20], P(('shard', 'rep'))
- grad_decay: bfloat16 [4096, 20], P(('shard', 'rep'))
- grad_conv: float32 [3, 4, 2560], replicated
- grad_alog: float32 [20], replicated
- grad_bias: float32 [20], replicated
- grad_gain: float32 [128], replicated
- grad_out_weight: float32 [2560, 2560], P('shard')
The draws below stay inside these ranges and needn't reach their ends.
All inputs are finite; a program needn't handle non-finite values.
Results may differ from the reference program's by a relative error of at most 0.012.
Values may be sent and summed in bfloat16 or wider, within the bound.
A program may use at most 256 MiB of HBM per device.

```python
import jax
import jax.numpy as jnp
from jax import lax

D = 2560
HEADS = 20
DK = 128
CONV = 4
TOK_DEV = 128
HK = 2560
TOKENS = 4096


def block_levels(rng, shape, cuts, smallest, top_value):
    gain, own = 1.0, jax.random.fold_in(rng, 6)
    for dim, blocks in cuts:
        heights = jnp.exp(jax.random.uniform(jax.random.fold_in(own, dim), (blocks,), jnp.float32, smallest / len(cuts), top_value / len(cuts)))
        gain = gain * jnp.repeat(heights, shape[dim] // blocks).reshape([-1 if axis == dim else 1 for axis in range(len(shape))])
    return gain


def noise(stream_key, shape, scale, bound, shards=(), held_as=jnp.bfloat16):
    values = scale * jax.random.normal(stream_key, shape, jnp.float32)
    if shards:
        values = values * block_levels(stream_key, shape, shards, -0.22, 0.18)
    return jnp.clip(values, -bound, bound).astype(held_as)


def setup_inputs(seed: int = 0) -> dict:
    streams_of = jax.random.split(jax.random.key(seed), 13)
    return {
        "queries_in": noise(streams_of[0], (TOKENS, HK), 1.0, 6.0, ((0, 32),)),
        "keys_in": noise(streams_of[1], (TOKENS, HK), 1.0, 6.0, ((0, 32),)),
        "values_in": noise(streams_of[2], (TOKENS, HK), 1.0, 6.0, ((0, 32),)),
        "gate_z": noise(streams_of[3], (TOKENS, HK), 1.0, 6.0, ((0, 32),)),
        "beta_logit": noise(streams_of[4], (TOKENS, HEADS), 1.5, 6.0, ((0, 32),)),
        "decay_in": noise(streams_of[5], (TOKENS, HEADS), 1.0, 6.0, ((0, 32),)),
        "a_log": jnp.clip(jax.random.uniform(streams_of[6], (HEADS,), jnp.float32, -4.5, 0.5), -4.5, 0.5),
        "dt_bias": jnp.clip(jax.random.uniform(streams_of[7], (HEADS,), jnp.float32, -2.0, 1.0), -2.0, 1.0),
        "conv_weight": noise(streams_of[8], (3, CONV, HK), 0.5, 3.0, (), jnp.float32),
        "norm_gain": jnp.clip(1.0 + 0.18 * jax.random.normal(streams_of[9], (DK,), jnp.float32), 0.1, 1.9),
        "out_weight": noise(streams_of[10], (HK, D), HK ** -0.5, 0.125, ((0, 16),)),
        "out_grad": noise(streams_of[11], (TOKENS, D), 1.0, 6.0, ((0, 32),)),
    }


def causal_conv(signal, kernel):
    extent = kernel.shape[0]
    length = signal.shape[0]
    padded = jnp.pad(signal, ((extent - 1, 0), (0, 0)))
    summed = kernel[0] * padded[0:length]
    for offset in range(1, extent):
        summed = summed + kernel[offset] * padded[offset:offset + length]
    return jax.nn.silu(summed)

def unit_heads(field):
    shaped = field.reshape(field.shape[0], HEADS, DK)
    return shaped * lax.rsqrt(lax.optimization_barrier(jnp.sum(shaped * shaped, axis=-1, keepdims=True)) + 1e-06)

def prepare(queries_in, keys_in, values_in, beta_logit, decay_in, conv_weight, a_log, dt_bias):
    queries = unit_heads(causal_conv(queries_in.astype(jnp.float32), conv_weight[0])) * DK ** (-0.5)
    keys = unit_heads(causal_conv(keys_in.astype(jnp.float32), conv_weight[1]))
    values = causal_conv(values_in.astype(jnp.float32), conv_weight[2]).reshape(values_in.shape[0], HEADS, DK)
    betas = jax.nn.sigmoid(beta_logit.astype(jnp.float32))
    decays = -jnp.exp(a_log) * jax.nn.softplus(decay_in.astype(jnp.float32) + dt_bias)
    return (queries, keys, values, betas, decays)

def finish(mixed, gate_z, norm_gain):
    normed = mixed * lax.rsqrt(lax.optimization_barrier(jnp.mean(mixed * mixed, axis=-1, keepdims=True)) + 1e-06) * norm_gain
    gates = jax.nn.silu(gate_z.astype(jnp.float32)).reshape(gate_z.shape[0], HEADS, DK)
    return (normed * gates).reshape(gate_z.shape[0], HEADS * DK)

def recur(queries, keys, values, betas, decays):

    def advance(state, inputs):
        query, key, value, beta, decay = inputs
        state = jnp.exp(decay)[:, None, None] * state
        predicted = jnp.einsum('hvk,hk->hv', state, key, precision=lax.Precision.HIGHEST)
        state = state + (beta[:, None] * (value - predicted))[:, :, None] * key[:, None, :]
        return (state, jnp.einsum('hvk,hk->hv', state, query, precision=lax.Precision.HIGHEST))
    start = jnp.zeros((HEADS, DK, DK), jnp.float32)
    _, mixed = lax.scan(advance, start, (queries, keys, values, betas, decays))
    return mixed

def mixer(queries_in, keys_in, values_in, gate_z, beta_logit, decay_in, conv_weight, a_log, dt_bias, norm_gain):
    queries, keys, values, betas, decays = prepare(queries_in, keys_in, values_in, beta_logit, decay_in, conv_weight, a_log, dt_bias)
    return finish(recur(queries, keys, values, betas, decays), gate_z, norm_gain)

def reference(queries_in, keys_in, values_in, gate_z, beta_logit, decay_in, a_log, dt_bias, conv_weight, norm_gain, out_weight, out_grad):
    documents = queries_in.shape[0] // TOK_DEV

    def split(field):
        return field.reshape((documents, TOK_DEV) + field.shape[1:])

    def one_document(carry, inputs):
        query_doc, key_doc, value_doc, gate_doc, beta_doc, decay_doc, grad_doc = inputs

        def local(qa, ka, va, za, ba, da, cw, al, db, gn):
            return mixer(qa, ka, va, za, ba, da, cw, al, db, gn)
        hidden_f, pullback = jax.vjp(local, query_doc, key_doc, value_doc, gate_doc, beta_doc, decay_doc, conv_weight, a_log, dt_bias, norm_gain)
        hidden = hidden_f.astype(jnp.bfloat16)
        output = jnp.dot(hidden, out_weight, preferred_element_type=jnp.float32).astype(jnp.bfloat16)
        grad_hidden = jnp.dot(grad_doc, out_weight.T, preferred_element_type=jnp.float32).astype(jnp.bfloat16)
        grads = pullback(grad_hidden.astype(jnp.float32))
        weight_acc = carry[0] + jnp.dot(hidden.T, grad_doc, preferred_element_type=jnp.float32)
        new_carry = (weight_acc, carry[1] + grads[6], carry[2] + grads[7], carry[3] + grads[8], carry[4] + grads[9])
        return (new_carry, (output, grads[0], grads[1], grads[2], grads[3], grads[4], grads[5]))
    start = (jnp.zeros(out_weight.shape, jnp.float32), jnp.zeros(conv_weight.shape, jnp.float32), jnp.zeros(a_log.shape, jnp.float32), jnp.zeros(dt_bias.shape, jnp.float32), jnp.zeros(norm_gain.shape, jnp.float32))
    carry, stacked = lax.scan(one_document, start, (split(queries_in), split(keys_in), split(values_in), split(gate_z), split(beta_logit), split(decay_in), split(out_grad)))
    merged = [field.reshape((documents * TOK_DEV,) + field.shape[2:]) for field in stacked]
    return (merged[0], merged[1], merged[2], merged[3], merged[4], merged[5], merged[6], carry[1], carry[2], carry[3], carry[4], carry[0])
```

```python
import functools

import jax
import jax.numpy as jnp
from jax import lax
from jax.experimental import pallas as pl
from jax.experimental.pallas import tpu as pltpu
from jax.sharding import PartitionSpec as P

DK = 128
STEP_HEADS = 4
EPS = 1e-06
F32 = jnp.float32
BF16 = jnp.bfloat16


def split(x):
    high = x.astype(BF16)
    return high, (x - high.astype(F32)).astype(BF16)


def mm(a, b):
    left = jnp.concatenate([a[0], a[0], a[1]], axis=1)
    right = jnp.concatenate([b[0], b[1], b[0]], axis=0)
    return jnp.dot(left, right, preferred_element_type=F32)


def mm_t(a, b):
    left = jnp.concatenate([a[0], a[0], a[1]], axis=1)
    right = jnp.concatenate([b[0], b[1], b[0]], axis=1)
    return lax.dot_general(left, right, (((1,), (1,)), ((), ())), preferred_element_type=F32)


def shift_down(x, count):
    if count == 0:
        return x
    rows = lax.broadcasted_iota(jnp.int32, x.shape, 0)
    return jnp.where(rows >= count, pltpu.roll(x, count, 0), 0.0)


def shift_up(x, count):
    if count == 0:
        return x
    rows = lax.broadcasted_iota(jnp.int32, x.shape, 0)
    size = x.shape[0]
    return jnp.where(rows < size - count, pltpu.roll(x, size - count, 0), 0.0)


def conv(x, w):
    taps = w.shape[0]
    total = w[0:1] * shift_down(x, taps - 1)
    for j in range(1, taps):
        total = total + w[j : j + 1] * shift_down(x, taps - 1 - j)
    return total


def sigmoid(x):
    return 1.0 / (1.0 + jnp.exp(-x))


def softplus(x):
    return jnp.maximum(x, 0.0) + jnp.log1p(jnp.exp(-jnp.abs(x)))


def grids(size):
    rows = lax.broadcasted_iota(jnp.int32, (size, size), 0)
    cols = lax.broadcasted_iota(jnp.int32, (size, size), 1)
    return rows, cols


def invert(system, rows, cols):
    size = system.shape[0]
    eye = (rows == cols).astype(F32)

    def corner(block):
        keep = (rows // (2 * block) == cols // (2 * block)) & (rows // block > cols // block)
        return jnp.where(keep, system, 0.0)

    inverse = eye - corner(1)
    block = 2
    while block < size:
        parts = split(inverse)
        inverse = inverse - mm(parts, split(mm(split(corner(block)), parts)))
        block *= 2
    return inverse


def gates(beta_ref, decay_ref, alog_ref, bias_ref):
    beta = sigmoid(beta_ref[...].astype(F32))
    logit = decay_ref[...].astype(F32) + bias_ref[...]
    decay = -jnp.exp(alog_ref[...]) * softplus(logit)
    return beta, logit, decay


def running(decay, rows, cols):
    lower = (rows >= cols).astype(F32)
    return jnp.dot(lower, decay, precision=lax.Precision.HIGHEST, preferred_element_type=F32)


def column(field, head):
    lanes = lax.broadcasted_iota(jnp.int32, field.shape, 1)
    return jnp.sum(jnp.where(lanes == head, field, 0.0), axis=1, keepdims=True)


def forward(xq, xk, xv, wq, wk, wv, beta, total, rows, cols):
    pq, pk, pv = conv(xq, wq), conv(xk, wk), conv(xv, wv)
    sq, sk, sv = sigmoid(pq), sigmoid(pk), sigmoid(pv)
    yq, yk, value = pq * sq, pk * sk, pv * sv
    rq = lax.rsqrt(jnp.sum(yq * yq, axis=1, keepdims=True) + EPS)
    rk = lax.rsqrt(jnp.sum(yk * yk, axis=1, keepdims=True) + EPS)
    query, key = yq * rq, yk * rk
    query_s, key_s = split(query * DK**-0.5), split(key)
    total_row = jnp.sum(jnp.where(rows == cols, total, 0.0), axis=0, keepdims=True)
    lower = rows >= cols
    weights = jnp.where(lower, jnp.exp(jnp.where(lower, total - total_row, 0.0)), 0.0)
    key_dots = mm_t(key_s, key_s)
    query_dots = mm_t(query_s, key_s)
    strict = jnp.where(rows > cols, weights, 0.0)
    inverse = invert(beta * strict * key_dots, rows, cols)
    corrected = mm(split(inverse), split(beta * value))
    mixing = weights * query_dots
    mixed = mm(split(mixing), split(corrected))
    return mixed, (
        (pq, pk, pv), (sq, sk, sv), value, (rq, rk), (query, key), (query_s, key_s),
        weights, strict, key_dots, mixing, inverse, corrected,
    )


def hidden_kernel(
    q_ref, k_ref, v_ref, z_ref, beta_ref, decay_ref, alog_ref, bias_ref, conv_ref, gain_ref, out_ref
):
    size = q_ref.shape[0]
    rows, cols = grids(size)
    betas, _, decay = gates(beta_ref, decay_ref, alog_ref, bias_ref)
    totals = running(decay, rows, cols)
    first = pl.program_id(0) * STEP_HEADS
    for i in range(STEP_HEADS):
        at = slice(i * DK, (i + 1) * DK)
        mixed, _ = forward(
            q_ref[:, at].astype(F32), k_ref[:, at].astype(F32), v_ref[:, at].astype(F32),
            conv_ref[0, :, at], conv_ref[1, :, at], conv_ref[2, :, at],
            column(betas, first + i), column(totals, first + i), rows, cols,
        )
        z = z_ref[:, at].astype(F32)
        r = lax.rsqrt(jnp.mean(mixed * mixed, axis=1, keepdims=True) + EPS)
        out_ref[:, at] = (mixed * r * gain_ref[...] * (z * sigmoid(z))).astype(BF16)


def silu_slope(p, s):
    return s * (1.0 + p * (1.0 - s))


def grads_kernel(
    q_ref, k_ref, v_ref, z_ref, beta_ref, decay_ref, alog_ref, bias_ref, conv_ref, gain_ref, gh_ref,
    gq_ref, gk_ref, gv_ref, gz_ref, gbeta_ref, gdecay_ref, gconv_ref, galog_ref, gbias_ref, ggain_ref,
    dbeta_acc, ddecay_acc,
):
    size = q_ref.shape[0]
    rows, cols = grids(size)
    betas, logit, decay = gates(beta_ref, decay_ref, alog_ref, bias_ref)
    totals = running(decay, rows, cols)
    step = pl.program_id(0)
    first = step * STEP_HEADS

    @pl.when(step == 0)
    def _():
        dbeta_acc[...] = jnp.zeros_like(dbeta_acc)
        ddecay_acc[...] = jnp.zeros_like(ddecay_acc)
        ggain_ref[...] = jnp.zeros_like(ggain_ref)

    lanes = lax.broadcasted_iota(jnp.int32, betas.shape, 1)
    gain = gain_ref[...]
    dbeta_all = jnp.zeros(betas.shape, F32)
    dtotal_all = jnp.zeros(betas.shape, F32)
    dgain = jnp.zeros_like(gain)
    for i in range(STEP_HEADS):
        at = slice(i * DK, (i + 1) * DK)
        xs = (q_ref[:, at].astype(F32), k_ref[:, at].astype(F32), v_ref[:, at].astype(F32))
        ws = (conv_ref[0, :, at], conv_ref[1, :, at], conv_ref[2, :, at])
        beta = column(betas, first + i)
        mixed, saved = forward(*xs, *ws, beta, column(totals, first + i), rows, cols)
        ps, ss, value, (rq, rk), (query, key), (query_s, key_s) = saved[:6]
        weights, strict, key_dots, mixing, inverse, corrected = saved[6:]

        z = z_ref[:, at].astype(F32)
        sz = sigmoid(z)
        gh = gh_ref[:, at].astype(F32)
        r = lax.rsqrt(jnp.mean(mixed * mixed, axis=1, keepdims=True) + EPS)
        unit = mixed * r
        gz_ref[:, at] = (gh * unit * gain * silu_slope(z, sz)).astype(BF16)
        dnorm = gh * (z * sz)
        dgain = dgain + jnp.sum(dnorm * unit, axis=0, keepdims=True)
        dunit = dnorm * gain
        dmixed = r * (dunit - unit * jnp.mean(unit * dunit, axis=1, keepdims=True))

        dmixed_s = split(dmixed)
        corrected_s = split(corrected)
        dmixing = mm_t(dmixed_s, corrected_s)
        dcorrected = mm(split(mixing.T), dmixed_s)
        drhs = mm(split(inverse.T), split(dcorrected))
        dsystem = -mm_t(split(drhs), corrected_s)
        dvalue = beta * drhs
        swept = dsystem * strict * key_dots
        dbeta = jnp.sum(drhs * value, axis=1, keepdims=True) + jnp.sum(swept, axis=1, keepdims=True)
        flow = dmixing * mixing + beta * swept
        flow_cols = jnp.sum(flow, axis=0, keepdims=True)
        flow_col = jnp.sum(jnp.where(rows == cols, flow_cols, 0.0), axis=1, keepdims=True)
        dtotal = jnp.sum(flow, axis=1, keepdims=True) - flow_col
        ddots = dmixing * weights
        pair = beta * dsystem * strict
        dquery = mm(split(ddots), key_s) * DK**-0.5
        dkey = mm(split(ddots.T), query_s) + mm(split(pair + pair.T), key_s)

        here = lanes == first + i
        dbeta_all = dbeta_all + jnp.where(here, dbeta, 0.0)
        dtotal_all = dtotal_all + jnp.where(here, dtotal, 0.0)

        dyq = rq * (dquery - query * jnp.sum(query * dquery, axis=1, keepdims=True))
        dyk = rk * (dkey - key * jnp.sum(key * dkey, axis=1, keepdims=True))
        for kind, (dy, ref) in enumerate(((dyq, gq_ref), (dyk, gk_ref), (dvalue, gv_ref))):
            dp = dy * silu_slope(ps[kind], ss[kind])
            w = ws[kind]
            taps = w.shape[0]
            dx = w[taps - 1 : taps] * dp
            for j in range(taps - 1):
                dx = dx + w[j : j + 1] * shift_up(dp, taps - 1 - j)
            ref[:, at] = dx.astype(BF16)
            for j in range(taps):
                gconv_ref[kind, j : j + 1, at] = jnp.sum(
                    dp * shift_down(xs[kind], taps - 1 - j), axis=0, keepdims=True
                )

    upper = (rows <= cols).astype(F32)
    dbeta_acc[...] += dbeta_all
    ddecay_acc[...] += jnp.dot(
        upper, dtotal_all, precision=lax.Precision.HIGHEST, preferred_element_type=F32
    )
    ggain_ref[...] += dgain

    @pl.when(step == pl.num_programs(0) - 1)
    def _():
        gbeta_ref[...] = (dbeta_acc[...] * betas * (1.0 - betas)).astype(BF16)
        ddecay = ddecay_acc[...]
        dlogit = -jnp.exp(alog_ref[...]) * sigmoid(logit) * ddecay
        gdecay_ref[...] = dlogit.astype(BF16)
        galog_ref[...] = jnp.sum(ddecay * decay, axis=0, keepdims=True)
        gbias_ref[...] = jnp.sum(dlogit, axis=0, keepdims=True)


def specs(tokens, heads, taps):
    width = STEP_HEADS * DK
    wide = pl.BlockSpec((tokens, width), lambda i: (0, i))
    small = pl.BlockSpec((tokens, heads), lambda i: (0, 0))
    row = pl.BlockSpec((1, heads), lambda i: (0, 0))
    taps_spec = pl.BlockSpec((3, taps, width), lambda i: (0, 0, i))
    gain = pl.BlockSpec((1, DK), lambda i: (0, 0))
    return wide, small, row, taps_spec, gain


PARAMS = pltpu.CompilerParams(vmem_limit_bytes=48 * 2**20)


def run_hidden(q, k, v, z, beta, decay, alog, bias, conv_weight, gain):
    tokens, features = q.shape
    heads = beta.shape[1]
    wide, small, row, taps, gains = specs(tokens, heads, conv_weight.shape[1])
    return pl.pallas_call(
        hidden_kernel,
        grid=(heads // STEP_HEADS,),
        out_shape=jax.ShapeDtypeStruct((tokens, features), BF16),
        in_specs=[wide] * 4 + [small] * 2 + [row] * 2 + [taps, gains],
        out_specs=wide,
        compiler_params=PARAMS,
        cost_estimate=pl.CostEstimate(flops=2 * 10**10, bytes_accessed=4 * 10**6, transcendentals=0),
        name="hidden",
    )(q, k, v, z, beta, decay, alog, bias, conv_weight, gain)


def run_grads(q, k, v, z, beta, decay, alog, bias, conv_weight, gain, gh):
    tokens, features = q.shape
    heads = beta.shape[1]
    wide, small, row, taps, gains = specs(tokens, heads, conv_weight.shape[1])
    big = jax.ShapeDtypeStruct((tokens, features), BF16)
    little = jax.ShapeDtypeStruct((tokens, heads), BF16)
    line = jax.ShapeDtypeStruct((1, heads), F32)
    return pl.pallas_call(
        grads_kernel,
        grid=(heads // STEP_HEADS,),
        out_shape=[big] * 4 + [little] * 2
        + [jax.ShapeDtypeStruct(conv_weight.shape, F32), line, line, jax.ShapeDtypeStruct((1, DK), F32)],
        in_specs=[wide] * 4 + [small] * 2 + [row] * 2 + [taps, gains, wide],
        out_specs=[wide] * 4 + [small] * 2 + [taps, row, row, gains],
        scratch_shapes=[pltpu.VMEM((tokens, heads), F32), pltpu.VMEM((tokens, heads), F32)],
        compiler_params=PARAMS,
        cost_estimate=pl.CostEstimate(flops=4 * 10**10, bytes_accessed=8 * 10**6, transcendentals=0),
        name="grads",
    )(q, k, v, z, beta, decay, alog, bias, conv_weight, gain, gh)


def sum_rep(part, size):
    if size == 2:
        return part + lax.ppermute(part, "rep", [(0, 1), (1, 0)])
    return lax.psum(part, "rep")


def shards(
    reps, queries_in, keys_in, values_in, gate_z, beta_logit, decay_in, a_log, dt_bias,
    conv_weight, norm_gain, out_weight, out_grad,
):
    inputs = (
        queries_in, keys_in, values_in, gate_z, beta_logit, decay_in,
        a_log[None, :], dt_bias[None, :], conv_weight, norm_gain[None, :],
    )
    gathered = lax.all_gather(out_weight, "shard", axis=0, tiled=True)
    hidden = run_hidden(*inputs)
    hidden_all = lax.all_to_all(hidden, "shard", split_axis=1, concat_axis=0, tiled=True)
    grad_all = lax.all_gather(out_grad, "shard", axis=0, tiled=True)
    grad_hidden = lax.dot_general(
        out_grad, gathered, (((1,), (1,)), ((), ())), preferred_element_type=F32
    ).astype(BF16)
    grads = run_grads(*inputs, grad_hidden)
    layer_out = jnp.dot(hidden, gathered, preferred_element_type=F32).astype(BF16)
    packed = jnp.concatenate(
        [grads[6].reshape(-1), grads[7].reshape(-1), grads[8].reshape(-1), grads[9].reshape(-1)]
    )
    packed = lax.psum(packed, ("shard", "rep"))
    own = lax.dot_general(
        hidden_all, grad_all, (((0,), (0,)), ((), ())), preferred_element_type=F32
    )
    grad_out_weight = sum_rep(own, reps)
    n_conv, heads = conv_weight.size, a_log.shape[0]
    return (
        layer_out, grads[0], grads[1], grads[2], grads[3], grads[4], grads[5],
        packed[:n_conv].reshape(conv_weight.shape),
        packed[n_conv : n_conv + heads],
        packed[n_conv + heads : n_conv + 2 * heads],
        packed[n_conv + 2 * heads :],
        grad_out_weight,
    )


def solution(mesh):
    rows = P(("shard", "rep"), None)
    return jax.shard_map(
        functools.partial(shards, mesh.shape["rep"]),
        mesh=mesh,
        in_specs=(rows,) * 6 + (P(), P(), P(), P(), P("shard", None), rows),
        out_specs=(rows,) * 7 + (P(), P(), P(), P(), P("shard", None)),
        check_vma=False,
    )
```

```python
import functools

import jax
import jax.numpy as jnp
from jax import lax
from jax.experimental import pallas as pl
from jax.experimental.pallas import tpu as pltpu
from jax.sharding import PartitionSpec as P

DK = 128
STEP_HEADS = 4
EPS = 1e-06
F32 = jnp.float32
BF16 = jnp.bfloat16


def split(x):
    high = x.astype(BF16)
    return high, (x - high.astype(F32)).astype(BF16)


def mm(a, b):
    left = jnp.concatenate([a[0], a[0], a[1]], axis=1)
    right = jnp.concatenate([b[0], b[1], b[0]], axis=0)
    return jnp.dot(left, right, preferred_element_type=F32)


def mm_t(a, b):
    left = jnp.concatenate([a[0], a[0], a[1]], axis=1)
    right = jnp.concatenate([b[0], b[1], b[0]], axis=1)
    return lax.dot_general(left, right, (((1,), (1,)), ((), ())), preferred_element_type=F32)


def shift_down(x, count):
    if count == 0:
        return x
    rows = lax.broadcasted_iota(jnp.int32, x.shape, 0)
    return jnp.where(rows >= count, pltpu.roll(x, count, 0), 0.0)


def shift_up(x, count):
    if count == 0:
        return x
    rows = lax.broadcasted_iota(jnp.int32, x.shape, 0)
    size = x.shape[0]
    return jnp.where(rows < size - count, pltpu.roll(x, size - count, 0), 0.0)


def conv(x, w):
    taps = w.shape[0]
    total = w[0:1] * shift_down(x, taps - 1)
    for j in range(1, taps):
        total = total + w[j : j + 1] * shift_down(x, taps - 1 - j)
    return total


def sigmoid(x):
    return 1.0 / (1.0 + jnp.exp(-x))


def softplus(x):
    return jnp.maximum(x, 0.0) + jnp.log1p(jnp.exp(-jnp.abs(x)))


def grids(size):
    rows = lax.broadcasted_iota(jnp.int32, (size, size), 0)
    cols = lax.broadcasted_iota(jnp.int32, (size, size), 1)
    return rows, cols


def invert(system, rows, cols):
    size = system.shape[0]
    eye = (rows == cols).astype(F32)

    def corner(block):
        keep = (rows // (2 * block) == cols // (2 * block)) & (rows // block > cols // block)
        return jnp.where(keep, system, 0.0)

    inverse = eye - corner(1)
    block = 2
    while block < size:
        parts = split(inverse)
        inverse = inverse - mm(parts, split(mm(split(corner(block)), parts)))
        block *= 2
    return inverse


def gates(beta_ref, decay_ref, alog_ref, bias_ref):
    beta = sigmoid(beta_ref[...].astype(F32))
    logit = decay_ref[...].astype(F32) + bias_ref[...]
    decay = -jnp.exp(alog_ref[...]) * softplus(logit)
    return beta, logit, decay


def running(decay, rows, cols):
    lower = (rows >= cols).astype(F32)
    return jnp.dot(lower, decay, precision=lax.Precision.HIGHEST, preferred_element_type=F32)


def column(field, head):
    lanes = lax.broadcasted_iota(jnp.int32, field.shape, 1)
    return jnp.sum(jnp.where(lanes == head, field, 0.0), axis=1, keepdims=True)


def forward(xq, xk, xv, wq, wk, wv, beta, total, rows, cols):
    pq, pk, pv = conv(xq, wq), conv(xk, wk), conv(xv, wv)
    sq, sk, sv = sigmoid(pq), sigmoid(pk), sigmoid(pv)
    yq, yk, value = pq * sq, pk * sk, pv * sv
    rq = lax.rsqrt(jnp.sum(yq * yq, axis=1, keepdims=True) + EPS)
    rk = lax.rsqrt(jnp.sum(yk * yk, axis=1, keepdims=True) + EPS)
    query, key = yq * rq, yk * rk
    query_s, key_s = split(query * DK**-0.5), split(key)
    total_row = jnp.sum(jnp.where(rows == cols, total, 0.0), axis=0, keepdims=True)
    lower = rows >= cols
    weights = jnp.where(lower, jnp.exp(jnp.where(lower, total - total_row, 0.0)), 0.0)
    key_dots = mm_t(key_s, key_s)
    query_dots = mm_t(query_s, key_s)
    strict = jnp.where(rows > cols, weights, 0.0)
    inverse = invert(beta * strict * key_dots, rows, cols)
    corrected = mm(split(inverse), split(beta * value))
    mixing = weights * query_dots
    mixed = mm(split(mixing), split(corrected))
    return mixed, (
        (pq, pk, pv), (sq, sk, sv), value, (rq, rk), (query, key), (query_s, key_s),
        weights, strict, key_dots, mixing, inverse, corrected,
    )


def hidden_kernel(
    q_ref, k_ref, v_ref, z_ref, beta_ref, decay_ref, alog_ref, bias_ref, conv_ref, gain_ref, out_ref
):
    size = q_ref.shape[0]
    rows, cols = grids(size)
    betas, _, decay = gates(beta_ref, decay_ref, alog_ref, bias_ref)
    totals = running(decay, rows, cols)
    first = pl.program_id(0) * STEP_HEADS
    for i in range(STEP_HEADS):
        at = slice(i * DK, (i + 1) * DK)
        mixed, _ = forward(
            q_ref[:, at].astype(F32), k_ref[:, at].astype(F32), v_ref[:, at].astype(F32),
            conv_ref[0, :, at], conv_ref[1, :, at], conv_ref[2, :, at],
            column(betas, first + i), column(totals, first + i), rows, cols,
        )
        z = z_ref[:, at].astype(F32)
        r = lax.rsqrt(jnp.mean(mixed * mixed, axis=1, keepdims=True) + EPS)
        out_ref[:, at] = (mixed * r * gain_ref[...] * (z * sigmoid(z))).astype(BF16)


def silu_slope(p, s):
    return s * (1.0 + p * (1.0 - s))


def grads_kernel(
    q_ref, k_ref, v_ref, z_ref, beta_ref, decay_ref, alog_ref, bias_ref, conv_ref, gain_ref, gh_ref,
    gq_ref, gk_ref, gv_ref, gz_ref, gbeta_ref, gdecay_ref, gconv_ref, galog_ref, gbias_ref, ggain_ref,
    dbeta_acc, ddecay_acc,
):
    size = q_ref.shape[0]
    rows, cols = grids(size)
    betas, logit, decay = gates(beta_ref, decay_ref, alog_ref, bias_ref)
    totals = running(decay, rows, cols)
    step = pl.program_id(0)
    first = step * STEP_HEADS

    @pl.when(step == 0)
    def _():
        dbeta_acc[...] = jnp.zeros_like(dbeta_acc)
        ddecay_acc[...] = jnp.zeros_like(ddecay_acc)
        ggain_ref[...] = jnp.zeros_like(ggain_ref)

    lanes = lax.broadcasted_iota(jnp.int32, betas.shape, 1)
    gain = gain_ref[...]
    dbeta_all = jnp.zeros(betas.shape, F32)
    dtotal_all = jnp.zeros(betas.shape, F32)
    dgain = jnp.zeros_like(gain)
    for i in range(STEP_HEADS):
        at = slice(i * DK, (i + 1) * DK)
        xs = (q_ref[:, at].astype(F32), k_ref[:, at].astype(F32), v_ref[:, at].astype(F32))
        ws = (conv_ref[0, :, at], conv_ref[1, :, at], conv_ref[2, :, at])
        beta = column(betas, first + i)
        mixed, saved = forward(*xs, *ws, beta, column(totals, first + i), rows, cols)
        ps, ss, value, (rq, rk), (query, key), (query_s, key_s) = saved[:6]
        weights, strict, key_dots, mixing, inverse, corrected = saved[6:]

        z = z_ref[:, at].astype(F32)
        sz = sigmoid(z)
        gh = gh_ref[:, at].astype(F32)
        r = lax.rsqrt(jnp.mean(mixed * mixed, axis=1, keepdims=True) + EPS)
        unit = mixed * r
        gz_ref[:, at] = (gh * unit * gain * silu_slope(z, sz)).astype(BF16)
        dnorm = gh * (z * sz)
        dgain = dgain + jnp.sum(dnorm * unit, axis=0, keepdims=True)
        dunit = dnorm * gain
        dmixed = r * (dunit - unit * jnp.mean(unit * dunit, axis=1, keepdims=True))

        dmixed_s = split(dmixed)
        corrected_s = split(corrected)
        dmixing = mm_t(dmixed_s, corrected_s)
        dcorrected = mm(split(mixing.T), dmixed_s)
        drhs = mm(split(inverse.T), split(dcorrected))
        dsystem = -mm_t(split(drhs), corrected_s)
        dvalue = beta * drhs
        swept = dsystem * strict * key_dots
        dbeta = jnp.sum(drhs * value, axis=1, keepdims=True) + jnp.sum(swept, axis=1, keepdims=True)
        flow = dmixing * mixing + beta * swept
        flow_cols = jnp.sum(flow, axis=0, keepdims=True)
        flow_col = jnp.sum(jnp.where(rows == cols, flow_cols, 0.0), axis=1, keepdims=True)
        dtotal = jnp.sum(flow, axis=1, keepdims=True) - flow_col
        ddots = dmixing * weights
        pair = beta * dsystem * strict
        dquery = mm(split(ddots), key_s) * DK**-0.5
        dkey = mm(split(ddots.T), query_s) + mm(split(pair + pair.T), key_s)

        here = lanes == first + i
        dbeta_all = dbeta_all + jnp.where(here, dbeta, 0.0)
        dtotal_all = dtotal_all + jnp.where(here, dtotal, 0.0)

        dyq = rq * (dquery - query * jnp.sum(query * dquery, axis=1, keepdims=True))
        dyk = rk * (dkey - key * jnp.sum(key * dkey, axis=1, keepdims=True))
        for kind, (dy, ref) in enumerate(((dyq, gq_ref), (dyk, gk_ref), (dvalue, gv_ref))):
            dp = dy * silu_slope(ps[kind], ss[kind])
            w = ws[kind]
            taps = w.shape[0]
            dx = w[taps - 1 : taps] * dp
            for j in range(taps - 1):
                dx = dx + w[j : j + 1] * shift_up(dp, taps - 1 - j)
            ref[:, at] = dx.astype(BF16)
            for j in range(taps):
                gconv_ref[kind, j : j + 1, at] = jnp.sum(
                    dp * shift_down(xs[kind], taps - 1 - j), axis=0, keepdims=True
                )

    upper = (rows <= cols).astype(F32)
    dbeta_acc[...] += dbeta_all
    ddecay_acc[...] += jnp.dot(
        upper, dtotal_all, precision=lax.Precision.HIGHEST, preferred_element_type=F32
    )
    ggain_ref[...] += dgain

    @pl.when(step == pl.num_programs(0) - 1)
    def _():
        gbeta_ref[...] = (dbeta_acc[...] * betas * (1.0 - betas)).astype(BF16)
        ddecay = ddecay_acc[...]
        dlogit = -jnp.exp(alog_ref[...]) * sigmoid(logit) * ddecay
        gdecay_ref[...] = dlogit.astype(BF16)
        galog_ref[...] = jnp.sum(ddecay * decay, axis=0, keepdims=True)
        gbias_ref[...] = jnp.sum(dlogit, axis=0, keepdims=True)


def specs(tokens, heads, taps):
    width = STEP_HEADS * DK
    wide = pl.BlockSpec((tokens, width), lambda i: (0, i))
    small = pl.BlockSpec((tokens, heads), lambda i: (0, 0))
    row = pl.BlockSpec((1, heads), lambda i: (0, 0))
    taps_spec = pl.BlockSpec((3, taps, width), lambda i: (0, 0, i))
    gain = pl.BlockSpec((1, DK), lambda i: (0, 0))
    return wide, small, row, taps_spec, gain


PARAMS = pltpu.CompilerParams(vmem_limit_bytes=48 * 2**20)


def run_hidden(q, k, v, z, beta, decay, alog, bias, conv_weight, gain):
    tokens, features = q.shape
    heads = beta.shape[1]
    wide, small, row, taps, gains = specs(tokens, heads, conv_weight.shape[1])
    return pl.pallas_call(
        hidden_kernel,
        grid=(heads // STEP_HEADS,),
        out_shape=jax.ShapeDtypeStruct((tokens, features), BF16),
        in_specs=[wide] * 4 + [small] * 2 + [row] * 2 + [taps, gains],
        out_specs=wide,
        compiler_params=PARAMS,
        cost_estimate=pl.CostEstimate(flops=6 * 10**10, bytes_accessed=4 * 10**6, transcendentals=0),
        name="hidden",
    )(q, k, v, z, beta, decay, alog, bias, conv_weight, gain)


def run_grads(q, k, v, z, beta, decay, alog, bias, conv_weight, gain, gh):
    tokens, features = q.shape
    heads = beta.shape[1]
    wide, small, row, taps, gains = specs(tokens, heads, conv_weight.shape[1])
    big = jax.ShapeDtypeStruct((tokens, features), BF16)
    little = jax.ShapeDtypeStruct((tokens, heads), BF16)
    line = jax.ShapeDtypeStruct((1, heads), F32)
    return pl.pallas_call(
        grads_kernel,
        grid=(heads // STEP_HEADS,),
        out_shape=[big] * 4 + [little] * 2
        + [jax.ShapeDtypeStruct(conv_weight.shape, F32), line, line, jax.ShapeDtypeStruct((1, DK), F32)],
        in_specs=[wide] * 4 + [small] * 2 + [row] * 2 + [taps, gains, wide],
        out_specs=[wide] * 4 + [small] * 2 + [taps, row, row, gains],
        scratch_shapes=[pltpu.VMEM((tokens, heads), F32), pltpu.VMEM((tokens, heads), F32)],
        compiler_params=PARAMS,
        cost_estimate=pl.CostEstimate(flops=8 * 10**10, bytes_accessed=8 * 10**6, transcendentals=0),
        name="grads",
    )(q, k, v, z, beta, decay, alog, bias, conv_weight, gain, gh)


def total_kernel(sizes, x_ref, out_ref, arrived, send_sem, recv_sem):
    names = tuple(sizes)
    where = {name: lax.axis_index(name) for name in names}
    partners = []
    for name in reversed(names):
        bit = 1
        while bit < sizes[name]:
            me = where[name]
            other = me + bit * (1 - 2 * lax.rem(me // bit, 2))
            partners.append(tuple(other if n == name else where[n] for n in names))
            bit *= 2
    barrier = pltpu.get_barrier_semaphore()
    for partner in partners:
        pl.semaphore_signal(barrier, inc=1, device_id=partner, device_id_type=pl.DeviceIdType.MESH)
    pl.semaphore_wait(barrier, len(partners))
    out_ref[...] = x_ref[...]
    for i, partner in enumerate(partners):
        copy = pltpu.make_async_remote_copy(
            src_ref=out_ref,
            dst_ref=arrived.at[i],
            send_sem=send_sem.at[i],
            recv_sem=recv_sem.at[i],
            device_id=partner,
            device_id_type=pl.DeviceIdType.MESH,
        )
        copy.start()
        copy.wait()
        out_ref[...] += arrived[i]


def run_total(x, sizes):
    rounds = sum(size.bit_length() - 1 for size in sizes.values())
    vmem = pl.BlockSpec(memory_space=pltpu.VMEM)
    return pl.pallas_call(
        functools.partial(total_kernel, sizes),
        out_shape=jax.ShapeDtypeStruct(x.shape, x.dtype),
        in_specs=[vmem],
        out_specs=vmem,
        scratch_shapes=[
            pltpu.VMEM((rounds, *x.shape), x.dtype),
            pltpu.SemaphoreType.DMA((rounds,)),
            pltpu.SemaphoreType.DMA((rounds,)),
        ],
        compiler_params=pltpu.CompilerParams(
            collective_id=0, has_side_effects=True, vmem_limit_bytes=16 * 2**20
        ),
        cost_estimate=pl.CostEstimate(flops=10**10, bytes_accessed=30 * 10**6, transcendentals=0),
        name="total",
    )(x)


def sum_rep(part, size):
    if size == 2:
        return part + lax.ppermute(part, "rep", [(0, 1), (1, 0)])
    return lax.psum(part, "rep")


def shards(
    sizes, queries_in, keys_in, values_in, gate_z, beta_logit, decay_in, a_log, dt_bias,
    conv_weight, norm_gain, out_weight, out_grad,
):
    inputs = (
        queries_in, keys_in, values_in, gate_z, beta_logit, decay_in,
        a_log[None, :], dt_bias[None, :], conv_weight, norm_gain[None, :],
    )
    reps = sizes["rep"]
    rep = lax.axis_index("rep")
    share = out_weight.shape[1] // reps
    mine = lax.all_gather(
        lax.dynamic_slice_in_dim(out_weight, rep * share, share, axis=1), "shard", axis=0, tiled=True
    )
    hidden = run_hidden(*inputs)
    out_grad_late, mine, hidden = lax.optimization_barrier((out_grad, mine, hidden))
    hidden_all = lax.all_to_all(hidden, "shard", split_axis=1, concat_axis=0, tiled=True)
    grad_all = lax.all_gather(out_grad_late, "shard", axis=0, tiled=True)
    parts = [mine] + [
        lax.ppermute(mine, "rep", [((i + k) % reps, i) for i in range(reps)]) for k in range(1, reps)
    ]
    back_dims = (((1,), (1,)), ((), ()))
    grad_hidden = sum(
        lax.dot_general(
            lax.dynamic_slice_in_dim(out_grad, lax.rem(rep + k, reps) * share, share, axis=1),
            part, back_dims, preferred_element_type=F32,
        )
        for k, part in enumerate(parts)
    ).astype(BF16)
    grads = run_grads(*inputs, grad_hidden)
    pieces = jnp.stack(
        [jnp.dot(hidden, part, preferred_element_type=F32).astype(BF16) for part in parts]
    )
    layer_out = jnp.concatenate(
        [
            lax.dynamic_index_in_dim(pieces, lax.rem(i - rep + reps, reps), 0, keepdims=False)
            for i in range(reps)
        ],
        axis=1,
    )
    small = jnp.concatenate([grads[i].reshape(-1) for i in range(6, 10)])
    filled = -small.size % (8 * 128)
    packed = run_total(jnp.pad(small, (0, filled)).reshape(-1, 128), sizes).reshape(-1)
    hidden_all, grad_all, packed, layer_out = lax.optimization_barrier(
        (hidden_all, grad_all, packed, layer_out)
    )
    own = lax.dot_general(
        hidden_all, grad_all, (((0,), (0,)), ((), ())), preferred_element_type=F32
    )
    grad_out_weight = sum_rep(own, reps)
    n_conv, heads = conv_weight.size, a_log.shape[0]
    gain_at = n_conv + 2 * heads
    return (
        layer_out, grads[0], grads[1], grads[2], grads[3], grads[4], grads[5],
        packed[:n_conv].reshape(conv_weight.shape),
        packed[n_conv : n_conv + heads],
        packed[n_conv + heads : gain_at],
        packed[gain_at : gain_at + norm_gain.size],
        grad_out_weight,
    )


def solution(mesh):
    rows = P(("shard", "rep"), None)
    return jax.shard_map(
        functools.partial(shards, dict(mesh.shape)),
        mesh=mesh,
        in_specs=(rows,) * 6 + (P(), P(), P(), P(), P("shard", None), rows),
        out_specs=(rows,) * 7 + (P(), P(), P(), P(), P("shard", None)),
        check_vma=False,
    )
```
